32 devices in a mesh: src: 16 (over z, y, core), tgt: 2 (over x).
Axes of the slice: x: 2, y: 2, z: 4, core: 2. Of those that a mesh axis runs over, the one named last changes fastest.
Arguments:
- atom_feats: bfloat16 [256, 3200], P(('src', 'tgt')), may hold values from -6 to 6
- positions: float32 [3, 256], P(None, ('src', 'tgt')), may hold values from 0 to 1
- edge_src: int32 [32768], P(('src', 'tgt')), may hold values from 0 to 15
- edge_tgt: int32 [32768], P(('src', 'tgt')), may hold values from 0 to 127
- edge_angle: float32 [32768], P(('src', 'tgt')), may hold values from -3.140625 to 3.140625
- edge_scale: float32 [32768], P(('src', 'tgt')), may hold values from 0.1 to 1
- edge_count: int32 [16, 2], replicated, may hold values from 1 to 1024, as said below
- k_index: int32 [3, 2048], replicated, may hold values from -6 to 6
- k_filter: float32 [2048, 128], replicated, may hold values from -6 to 6
- weight_zero: bfloat16 [2, 640, 640], replicated, may hold values from -0.25 to 0.25
- weight_first: bfloat16 [2, 2, 512, 512], replicated, may hold values from -0.1875 to 0.1875
- weight_second: bfloat16 [2, 2, 384, 384], replicated, may hold values from -0.21875 to 0.21875
- weight_third: bfloat16 [2, 2, 256, 256], replicated, may hold values from -0.25 to 0.25
- weight_fourth: bfloat16 [2, 2, 128, 128], replicated, may hold values from -0.375 to 0.375
Outputs:
- edge_update: bfloat16 [256, 3200], P(('tgt', 'src'))
- long_range: float32 [256, 128], P(('src', 'tgt'))
The draws below stay inside these ranges and needn't reach their ends.
Inputs may be any that keep to these rules, and one draw needn't show every extreme that they name: `edge_count`: live edge slots of tile (s, t); in every draw some tile is full with 1024.
All inputs are finite; a program needn't handle non-finite values.
Results may differ from the reference program's by a relative error of at most 0.0047.
Values may be sent and summed in bfloat16 or wider, within the bound.
A program may use at most 64 MiB of HBM per device.

```python
import math
import jax
import jax.numpy as jnp
from jax import lax

C = 128
LMAX = 4
FEATS = 3200
EDGE_CAP = 1024
KVECS = 2048
SRC_GROUPS = 16
TGT_GROUPS = 2
SRC_BLK = 16
TGT_BLK = 128
ATOMS = 256
EDGES = 32768
N_TGT = 2
DEVICES = 32


def draw_edge_count(key, part):
    base_key = jax.random.fold_in(key, 11)
    full_key = jax.random.fold_in(key, 12)
    tiles = SRC_GROUPS * TGT_GROUPS
    counts = jax.random.randint(base_key, (tiles,), EDGE_CAP // 8, EDGE_CAP // 2 + 1)
    chosen = jax.random.randint(full_key, (), 0, tiles)
    counts = jnp.where(jnp.arange(tiles) == chosen, EDGE_CAP, counts)
    return counts.reshape(SRC_GROUPS, TGT_GROUPS).astype(jnp.int32)


def with_ends(array, rng, low, high):
    index_at = [jax.random.randint(jax.random.fold_in(rng, axis), (), 0, length) for axis, length in enumerate(array.shape)]
    main_axis = array.shape.index(max(array.shape))
    beside = index_at[:main_axis] + [(index_at[main_axis] + 1) % array.shape[main_axis]] + index_at[main_axis + 1:]
    return array.at[tuple(index_at)].set(low).at[tuple(beside)].set(high)


def block_scale(key, dims, shards, smallest, top_value):
    def one(dim, parts):
        heights = jax.random.uniform(jax.random.fold_in(jax.random.fold_in(key, 6), dim), (parts,), jnp.float32, smallest / len(shards), top_value / len(shards))
        return jnp.repeat(jnp.exp(heights), dims[dim] // parts).reshape((-1,) + (1,) * (len(dims) - dim - 1))

    loudness = one(*shards[0])
    for cut in shards[1:]:
        loudness = loudness * one(*cut)
    return loudness


def gaussian(own_key, extent, scale, reach, shards=(), held_as=jnp.bfloat16):
    array = scale * jax.random.normal(own_key, extent, jnp.float32)
    if shards:
        array = array * block_scale(own_key, extent, shards, -0.22, 0.18)
    return jnp.clip(array, -reach, reach).astype(held_as)


def setup_inputs(seed: int = 0) -> dict:
    seeds = jax.random.split(jax.random.key(seed), 15)
    return {
        "atom_feats": gaussian(seeds[0], (ATOMS, FEATS), 1.0, 6.0, ((0, 32),)),
        "positions": jnp.clip(1.0 * jax.random.uniform(seeds[1], (3, ATOMS), jnp.float32) ** block_scale(seeds[1], (3, ATOMS), ((1, 32),), -0.2, 0.2), 0.0, 1.0),
        "edge_src": with_ends(jax.random.randint(seeds[2], (EDGES,), 0, SRC_BLK), jax.random.fold_in(seeds[2], 1), 0, SRC_BLK - 1).astype(jnp.int32),
        "edge_tgt": with_ends(jax.random.randint(seeds[3], (EDGES,), 0, TGT_BLK), jax.random.fold_in(seeds[3], 1), 0, TGT_BLK - 1).astype(jnp.int32),
        "edge_angle": jnp.clip(jax.random.uniform(seeds[4], (EDGES,), jnp.float32, -3.140625, 3.140625), -3.140625, 3.140625),
        "edge_scale": jnp.clip(jnp.exp(math.log(1.0) - 2.3025851 * jax.random.uniform(seeds[5], (EDGES,), jnp.float32) ** block_scale(seeds[5], (EDGES,), ((0, 32),), -0.2, 0.2)), 0.1, 1.0),
        "edge_count": draw_edge_count(jax.random.fold_in(seeds[14], 71), 0),
        "k_index": with_ends(jax.random.randint(seeds[7], (3, KVECS), -6, 7), jax.random.fold_in(seeds[7], 1), -6, 6).astype(jnp.int32),
        "k_filter": gaussian(seeds[8], (KVECS, C), 1.0, 6.0, (), jnp.float32),
        "weight_zero": gaussian(seeds[9], (2, (LMAX + 1) * C, (LMAX + 1) * C), ((LMAX + 1) * C) ** -0.5, 0.25),
        "weight_first": gaussian(seeds[10], (2, 2, LMAX * C, LMAX * C), (2 * LMAX * C) ** -0.5, 0.1875),
        "weight_second": gaussian(seeds[11], (2, 2, (LMAX - 1) * C, (LMAX - 1) * C), (2 * (LMAX - 1) * C) ** -0.5, 0.21875),
        "weight_third": gaussian(seeds[12], (2, 2, (LMAX - 2) * C, (LMAX - 2) * C), (2 * (LMAX - 2) * C) ** -0.5, 0.25),
        "weight_fourth": gaussian(seeds[13], (2, 2, (LMAX - 3) * C, (LMAX - 3) * C), (2 * (LMAX - 3) * C) ** -0.5, 0.375),
    }


def rotate(values, angles, handed):
    pieces = [values[:, :(LMAX + 1) * C]]
    offset = (LMAX + 1) * C
    for degree in range(1, LMAX + 1):
        columns = (LMAX + 1 - degree) * C
        cosine = jnp.cos(degree * angles)[:, None]
        sine_part = handed * jnp.sin(degree * angles)[:, None]
        leading = values[:, offset:offset + columns]
        trailing = values[:, offset + columns:offset + 2 * columns]
        pieces.append(cosine * leading + sine_part * trailing)
        pieces.append(cosine * trailing - sine_part * leading)
        offset += 2 * columns
    return jnp.concatenate(pieces, axis=1)

def pair_matrix(weights, conv_index):
    upper_half = jnp.concatenate([weights[conv_index, 0], weights[conv_index, 1]], axis=1)
    lower_half = jnp.concatenate([-weights[conv_index, 1], weights[conv_index, 0]], axis=1)
    return jnp.concatenate([upper_half, lower_half], axis=0)

def convolve(inputs, matrices):
    outputs = []
    offset = 0
    for matrix in matrices:
        height = matrix.shape[0]
        outputs.append(jnp.dot(inputs[:, offset:offset + height], matrix, preferred_element_type=jnp.float32))
        offset += height
    return jnp.concatenate(outputs, axis=1)

def edge_message(edge_rows, angles, scales, matrices_one, matrices_two):
    turned = rotate(edge_rows.astype(jnp.float32), angles, 1.0).astype(jnp.bfloat16)
    hidden = jax.nn.gelu(convolve(turned, matrices_one), approximate=False).astype(jnp.bfloat16)
    second = convolve(hidden, matrices_two)
    return rotate(second, angles, -1.0) * scales[:, None]

def reference(atom_feats, positions, edge_src, edge_tgt, edge_angle, edge_scale, edge_count, k_index, k_filter, weight_zero, weight_first, weight_second, weight_third, weight_fourth):
    sections = []
    for conv_index in (0, 1):
        sections.append([weight_zero[conv_index]] + [pair_matrix(weights, conv_index) for weights in (weight_first, weight_second, weight_third, weight_fourth)])
    slot_ids = jnp.arange(EDGE_CAP, dtype=jnp.int32)

    def add_tile(tile_index, totals):
        tile_index = tile_index.astype(jnp.int32)
        source_group = tile_index // N_TGT
        target_group = tile_index % N_TGT
        source_block = lax.dynamic_slice_in_dim(atom_feats, (source_group * SRC_BLK).astype(jnp.int32), SRC_BLK, 0)
        first_slot = (tile_index * EDGE_CAP).astype(jnp.int32)
        sources = lax.dynamic_slice_in_dim(edge_src, first_slot, EDGE_CAP)
        targets = lax.dynamic_slice_in_dim(edge_tgt, first_slot, EDGE_CAP)
        angles = lax.dynamic_slice_in_dim(edge_angle, first_slot, EDGE_CAP)
        scales = lax.dynamic_slice_in_dim(edge_scale, first_slot, EDGE_CAP)
        live_mask = (slot_ids < edge_count[source_group, target_group]).astype(jnp.float32)
        edge_rows = jnp.take(source_block, sources, axis=0)
        messages = edge_message(edge_rows, angles, scales, sections[0], sections[1]) * live_mask[:, None]
        partial_value = jax.ops.segment_sum(messages, targets, num_segments=TGT_BLK)
        row_start = (target_group * TGT_BLK).astype(jnp.int32)
        current = lax.dynamic_slice_in_dim(totals, row_start, TGT_BLK, 0)
        return lax.dynamic_update_slice_in_dim(totals, current + partial_value, row_start, 0)
    totals = lax.fori_loop(0, DEVICES, add_tile, jnp.zeros((ATOMS, FEATS), jnp.float32))
    edge_update = totals.astype(jnp.bfloat16)
    k_float = k_index.astype(jnp.float32)
    phase = 2.0 * math.pi * (positions[0][:, None] * k_float[0][None, :] + positions[1][:, None] * k_float[1][None, :] + positions[2][:, None] * k_float[2][None, :])
    cos_table = jnp.cos(phase)
    sin_table = jnp.sin(phase)
    charges = atom_feats[:, :C].astype(jnp.float32)
    factors_cos = jnp.dot(cos_table.T, charges, precision=lax.Precision.HIGHEST, preferred_element_type=jnp.float32)
    factors_sin = jnp.dot(sin_table.T, charges, precision=lax.Precision.HIGHEST, preferred_element_type=jnp.float32)
    summed = jnp.dot(cos_table, k_filter * factors_cos, precision=lax.Precision.HIGHEST, preferred_element_type=jnp.float32) + jnp.dot(sin_table, k_filter * factors_sin, precision=lax.Precision.HIGHEST, preferred_element_type=jnp.float32)
    long_range = summed * (1.0 / math.sqrt(ATOMS * KVECS))
    return (edge_update, long_range)
```

```python
import functools
import math

import jax
import jax.numpy as jnp
from jax import lax
from jax.experimental import pallas as pl
from jax.experimental.pallas import tpu as pltpu
from jax.sharding import PartitionSpec as P

MESH = pl.DeviceIdType.MESH
F32 = jnp.float32
BF16 = jnp.bfloat16
DEGREES = 4
ORDER_PLAN = (3, 1, 2, 0, 4)


def units_of(order):
    return (DEGREES + 2) // 2 if order == 0 else DEGREES + 1 - order


def first_unit(order):
    return sum(units_of(m) for m in range(order))


UNITS = first_unit(DEGREES + 1)


def first_block(order):
    return 0 if order == 0 else DEGREES + 1 + sum(2 * (DEGREES + 1 - m) for m in range(1, order))


def split(value):
    high = value.astype(BF16)
    return high, (value - high.astype(F32)).astype(BF16)


def half_turn(x):
    u = x * x
    s = x * (1 + u * (-1 / 6 + u * (1 / 120 + u * (-1 / 5040 + u * (1 / 362880 - u / 39916800)))))
    c = 1 + u * (
        -0.5
        + u * (1 / 24 + u * (-1 / 720 + u * (1 / 40320 + u * (-1 / 3628800 + u / 479001600))))
    )
    return 1 - 2 * s * s, 2 * s * c


def gelu(x):
    return 0.5 * x * (1 + lax.erf(x * math.sqrt(0.5)))


def dot(a, b):
    return jnp.dot(a, b, preferred_element_type=F32)


def kernel(
    sizes,
    x_ref, pos_ref, esrc_ref, etgt_ref, eang_ref, escale_ref, count_ref, kidx_ref, kfilt_hbm,
    w0_hbm, w1_hbm, w2_hbm, w3_hbm, w4_hbm,
    edge_out, long_out,
    xs, ew, w0, w1, w2, w3, w4, kfilt, y, e, t, h, send, recv,
    x_send, x_recv, ew_send, ew_recv, g_send, g_recv, w_sem,
):
    S, T, own, C, rows, sources, edges, kvecs = sizes
    N = S * T
    si, ti = lax.axis_index("src"), lax.axis_index("tgt")
    me = si * T + ti
    hbm = (w0_hbm, w1_hbm, w2_hbm, w3_hbm, w4_hbm)
    held = (w0, w1, w2, w3, w4)
    blocks = (DEGREES + 1) ** 2
    front = (blocks + 1) // 2

    weight_copies = []
    for conv in (0, 1):
        for m in range(DEGREES + 1):
            weight_copies.append(
                pltpu.make_async_copy(hbm[m].at[conv], held[m].at[conv], w_sem.at[conv, m])
            )
    for copy in weight_copies[: DEGREES + 1]:
        copy.start()
    filter_copy = pltpu.make_async_copy(kfilt_hbm, kfilt, w_sem.at[2, 0])

    barrier = pltpu.get_barrier_semaphore()

    def greet(d, _):
        p = lax.rem(me + d, N)
        pl.semaphore_signal(barrier, inc=1, device_id=(p // T, lax.rem(p, T)), device_id_type=MESH)
        return 0

    lax.fori_loop(1, N, greet, 0)

    xf = x_ref[...].astype(F32)
    tail = jnp.concatenate(
        [xf[:, front * C :], jnp.zeros((own, (2 * front - blocks) * C), F32)], axis=1
    )
    xs[ti] = jnp.concatenate([xf[:, : front * C], tail], axis=0).astype(BF16)
    lane = lax.broadcasted_iota(jnp.int32, (own, C), 1)
    diagonal = lax.broadcasted_iota(jnp.int32, (own, own), 0) == lax.broadcasted_iota(
        jnp.int32, (own, own), 1
    )
    placed = jnp.zeros((own, C), F32)
    own_columns = []
    for axis in range(3):
        column = jnp.sum(jnp.where(diagonal, pos_ref[axis : axis + 1, :], 0.0), axis=1, keepdims=True)
        own_columns.append(column)
        placed = jnp.where(lane == axis, column, placed)
    ew[me] = jnp.concatenate([xf[:, :C], placed], axis=0)

    pl.semaphore_wait(barrier, N - 1)

    def x_copy(slot, peer, there):
        return pltpu.make_async_remote_copy(
            src_ref=xs.at[slot], dst_ref=xs.at[slot], send_sem=x_send.at[peer],
            recv_sem=x_recv.at[there], device_id=(si, peer), device_id_type=MESH,
        )

    for d in range(1, T):
        x_copy(ti, lax.rem(ti + d, T), ti).start()

    def ew_copy(slot, p):
        return pltpu.make_async_remote_copy(
            src_ref=ew.at[slot], dst_ref=ew.at[slot], send_sem=ew_send.at[p],
            recv_sem=ew_recv.at[slot], device_id=(p // T, lax.rem(p, T)), device_id_type=MESH,
        )

    def ew_start(d, _):
        ew_copy(me, lax.rem(me + d, N)).start()
        return 0

    lax.fori_loop(1, N, ew_start, 0)
    for copy in weight_copies[DEGREES + 1 :]:
        copy.start()
    filter_copy.start()

    c1, s1 = half_turn(0.5 * eang_ref[...])
    c2, s2 = c1 * c1 - s1 * s1, 2 * s1 * c1
    c3, s3 = c2 * c1 - s2 * s1, s2 * c1 + c2 * s1
    c4, s4 = c2 * c2 - s2 * s2, 2 * s2 * c2
    cosines, sines = (None, c1, c2, c3, c4), (None, s1, s2, s3, s4)
    slots = lax.broadcasted_iota(jnp.int32, (1, edges), 1)
    scale = jnp.where(slots < count_ref[si, ti], escale_ref[...], 0.0)
    source_hot = lax.broadcasted_iota(jnp.int32, (sources, edges), 0) == esrc_ref[...]
    target_hot = lax.broadcasted_iota(jnp.int32, (rows, edges), 0) == etgt_ref[...]

    def put(hot, value):
        return jnp.where(hot, value, 0.0)

    def build_e(m):
        if m == 0:
            hot = put(source_hot, jnp.ones((1, edges), F32))
            parts = [hot, hot]
        else:
            ch, sh = cosines[m].astype(BF16).astype(F32), sines[m].astype(BF16).astype(F32)
            ch_hot, sh_hot = put(source_hot, ch), put(source_hot, sh)
            parts = [
                ch_hot, sh_hot, ch_hot, sh_hot,
                put(source_hot, cosines[m] - ch), put(source_hot, sines[m] - sh),
            ]
        depth = e.shape[1]
        used = len(parts) * sources
        if used < depth:
            parts.append(jnp.zeros((depth - used, edges), F32))
        e[...] = jnp.transpose(jnp.concatenate(parts, axis=0)).astype(BF16)

    def build_t(m):
        if m == 0:
            terms = [scale]
        else:
            terms = [scale * cosines[m], scale * sines[m]]
        count = len(terms)
        for i, term in enumerate(terms):
            high = term.astype(BF16).astype(F32)
            t[i * rows : (i + 1) * rows, :] = put(target_hot, high).astype(BF16)
            t[(count + i) * rows : (count + i + 1) * rows, :] = put(target_hot, term - high).astype(BF16)
        return count

    for d in range(1, T):
        peer = lax.rem(ti + d, T)
        x_copy(peer, peer, peer).wait_recv()
    for copy in weight_copies[: DEGREES + 1]:
        copy.wait()
    gathered = xs[...].astype(F32)

    def x_block(index):
        half, at = index // front, index % front
        piece = gathered[:, half * own : (half + 1) * own, at * C : (at + 1) * C]
        return piece.reshape(T * own, C)

    y[...] = jnp.zeros_like(y)
    for m in ORDER_PLAN:
        width = DEGREES + 1 - m
        base = first_block(m)
        if m == 0:
            left = jnp.concatenate([x_block(i) for i in range(width)], axis=1).astype(BF16)
            high, low = split(dot(left, w0[0]))
            for i in range(width):
                at = slice((i % 2) * C, (i % 2 + 1) * C)
                y[i // 2, 0:sources, at] = high[:, i * C : (i + 1) * C]
                y[i // 2, sources : 2 * sources, at] = low[:, i * C : (i + 1) * C]
        else:
            a = jnp.concatenate([x_block(base + i) for i in range(width)], axis=1)
            b = jnp.concatenate([x_block(base + width + i) for i in range(width)], axis=1)
            left = jnp.concatenate([a, b], axis=0).astype(BF16)
            by_w, by_v = dot(left, held[m][0, 0]), dot(left, held[m][0, 1])
            ya = by_w[:sources] - by_v[sources:]
            yb = by_v[:sources] + by_w[sources:]
            ah, al = split(ya)
            bh, bl = split(yb)
            for i in range(width):
                cut = slice(i * C, (i + 1) * C)
                unit = first_unit(m) + i
                for place, (p, q) in enumerate(
                    ((ah, bh), (bh, -ah), (al, bl), (bl, -al), (ah, bh), (bh, -ah))
                ):
                    at = slice(place * sources, (place + 1) * sources)
                    y[unit, at, 0:C] = p[:, cut]
                    y[unit, at, C : 2 * C] = q[:, cut]

    def g_copy(m, slot, p):
        span = pl.ds(first_unit(m), units_of(m))
        return pltpu.make_async_remote_copy(
            src_ref=send.at[p, span], dst_ref=recv.at[slot, span], send_sem=g_send.at[m, p],
            recv_sem=g_recv.at[m, slot], device_id=(p, ti), device_id_type=MESH,
        )

    step = 256
    for m in ORDER_PLAN:
        build_e(m)
        count = build_t(m)

        def one_unit(unit, _, count=count):
            for at in range(0, edges, step):
                h[at : at + step, :] = gelu(dot(e[at : at + step, :], y[unit])).astype(BF16)
            both = dot(t[0 : 2 * count * rows, :], h[...])
            total = both[: count * rows] + both[count * rows :]
            if count == 1:
                a, b = total[:, :C], total[:, C:]
            else:
                a = total[:rows, :C] - total[rows:, C:]
                b = total[:rows, C:] + total[rows:, :C]
            stacked = jnp.concatenate([a.reshape(S, own, C), b.reshape(S, own, C)], axis=1)
            send[:, pl.ds(unit, 1)] = stacked.astype(BF16)[:, None]
            return 0

        lax.fori_loop(first_unit(m), first_unit(m) + units_of(m), one_unit, 0)

        def g_start(d, _, m=m):
            g_copy(m, si, lax.rem(si + d, S)).start()
            return 0

        lax.fori_loop(1, S, g_start, 0)

    def ew_wait(d, _):
        p = lax.rem(me + d, N)
        copy = ew_copy(p, p)
        copy.wait_recv()
        return 0

    lax.fori_loop(1, N, ew_wait, 0)
    filter_copy.wait()
    k_step = 512
    some = math.gcd(N, 32)

    def tables(columns, at):
        turns = sum(
            column * kidx_ref[axis : axis + 1, pl.ds(at, k_step)].astype(F32)
            for axis, column in enumerate(columns)
        )
        return half_turn(math.pi * (turns - jnp.floor(turns + 0.5)))

    def k_chunk(number, total):
        at = pl.multiple_of(number * k_step, k_step)

        def atoms(group, carried):
            block = ew[pl.ds(group * some, some)]
            charges = jnp.transpose(block[:, :own].reshape(some * own, C)).astype(BF16)
            places = block[:, own:].reshape(some * own, C)
            made = tables([places[:, axis : axis + 1] for axis in range(3)], at)
            return tuple(
                held_sum + sum(dot(charges, part) for part in split(table))
                for held_sum, table in zip(carried, made)
            )

        zero = jnp.zeros((C, k_step), F32)
        if N == some:
            facts_here = atoms(0, (zero, zero))
        else:
            facts_here = lax.fori_loop(0, N // some, atoms, (zero, zero))
        filt = jnp.transpose(kfilt[pl.ds(at, k_step), :])
        for table, fact in zip(tables(own_columns, at), facts_here):
            th, tl = split(table)
            fh, fl = split(filt * fact)
            dims = (((1,), (1,)), ((), ()))
            for p, q in ((th, fh), (tl, fh), (th, fl)):
                total = total + lax.dot_general(p, q, dims, preferred_element_type=F32)
        return total

    summed = lax.fori_loop(0, kvecs // k_step, k_chunk, jnp.zeros((own, C), F32))
    long_out[...] = summed * (1.0 / math.sqrt(N * own * kvecs))

    for copy in weight_copies[DEGREES + 1 :]:
        copy.wait()
    for m in ORDER_PLAN:

        def g_wait(d, _, m=m):
            p = lax.rem(si + d, S)
            g_copy(m, p, p).wait_recv()
            return 0

        lax.fori_loop(1, S, g_wait, 0)
        span = pl.ds(first_unit(m), units_of(m))

        def g_add(d, total):
            return total + recv[lax.rem(si + d, S), span].astype(F32)

        total = lax.fori_loop(1, S, g_add, send[si, span].astype(F32))
        width = DEGREES + 1 - m
        base = first_block(m) * C
        if m == 0:
            left = jnp.concatenate(
                [total[i // 2, (i % 2) * own : (i % 2 + 1) * own] for i in range(width)], axis=1
            )
            by_w = dot(jnp.concatenate(split(left), axis=0), w0[1])
            edge_out[:, : width * C] = (by_w[:own] + by_w[own:]).astype(BF16)
        else:
            left = jnp.concatenate([total[i] for i in range(width)], axis=1)
            left = jnp.concatenate(split(left), axis=0)
            by_w, by_v = dot(left, held[m][1, 0]), dot(left, held[m][1, 1])
            by_w, by_v = (v[: 2 * own] + v[2 * own :] for v in (by_w, by_v))
            edge_out[:, base : base + width * C] = (by_w[:own] - by_v[own:]).astype(BF16)
            edge_out[:, base + width * C : base + 2 * width * C] = (by_v[:own] + by_w[own:]).astype(BF16)

    for d in range(1, T):
        peer = lax.rem(ti + d, T)
        x_copy(ti, peer, ti).wait_send()

    def ew_sent(d, _):
        ew_copy(me, lax.rem(me + d, N)).wait_send()
        return 0

    lax.fori_loop(1, N, ew_sent, 0)

    def g_sent(d, _):
        for m in ORDER_PLAN:
            g_copy(m, si, lax.rem(si + d, S)).wait_send()
        return 0

    lax.fori_loop(1, S, g_sent, 0)


def body(
    atom_feats, positions, edge_src, edge_tgt, edge_angle, edge_scale, edge_count, k_index, k_filter,
    weight_zero, weight_first, weight_second, weight_third, weight_fourth,
):
    S, T = lax.axis_size("src"), lax.axis_size("tgt")
    own, features = atom_feats.shape
    kvecs, C = k_filter.shape
    edges = edge_src.shape[0]
    rows, sources = own * S, own * T
    weights = (weight_zero, weight_first, weight_second, weight_third, weight_fourth)
    sizes = (S, T, own, C, rows, sources, edges, kvecs)
    depth = max(C, 6 * sources)
    front = ((DEGREES + 1) ** 2 + 1) // 2
    vmem = pl.BlockSpec(memory_space=pltpu.VMEM)
    smem = pl.BlockSpec(memory_space=pltpu.SMEM)
    anywhere = pl.BlockSpec(memory_space=pl.ANY)
    dma = pltpu.SemaphoreType.DMA
    row = lambda v: v.reshape(1, edges)
    return pl.pallas_call(
        functools.partial(kernel, sizes),
        out_shape=(
            jax.ShapeDtypeStruct((own, features), BF16),
            jax.ShapeDtypeStruct((own, C), F32),
        ),
        in_specs=[vmem] * 6 + [smem, vmem] + [anywhere] * 6,
        out_specs=(vmem, vmem),
        scratch_shapes=[
            pltpu.VMEM((T, 2 * own, front * C), BF16),
            pltpu.VMEM((S * T, 2 * own, C), F32),
            *[pltpu.VMEM(w.shape, BF16) for w in weights],
            pltpu.VMEM((kvecs, C), F32),
            pltpu.VMEM((UNITS, depth, 2 * C), BF16),
            pltpu.VMEM((edges, depth), BF16),
            pltpu.VMEM((4 * rows, edges), BF16),
            pltpu.VMEM((edges, 2 * C), BF16),
            pltpu.VMEM((S, UNITS, 2 * own, C), BF16),
            pltpu.VMEM((S, UNITS, 2 * own, C), BF16),
            dma((T,)), dma((T,)), dma((S * T,)), dma((S * T,)),
            dma((DEGREES + 1, S)), dma((DEGREES + 1, S)), dma((3, DEGREES + 1)),
        ],
        compiler_params=pltpu.CompilerParams(
            collective_id=0, has_side_effects=True, vmem_limit_bytes=56 * 1024 * 1024
        ),
    )(
        atom_feats, positions, row(edge_src), row(edge_tgt), row(edge_angle), row(edge_scale),
        edge_count, k_index, k_filter, *weights,
    )


def solution(mesh):
    both = P(("src", "tgt"))
    return jax.shard_map(
        body,
        mesh=mesh,
        in_specs=(
            P(("src", "tgt"), None), P(None, ("src", "tgt")), both, both, both, both,
            P(), P(), P(), P(), P(), P(), P(), P(),
        ),
        out_specs=(P(("tgt", "src"), None), P(("src", "tgt"), None)),
        check_vma=False,
    )
```

```python
import functools
import math

import jax
import jax.numpy as jnp
from jax import lax
from jax.experimental import pallas as pl
from jax.experimental.pallas import tpu as pltpu
from jax.sharding import PartitionSpec as P

MESH = pl.DeviceIdType.MESH
F32 = jnp.float32
BF16 = jnp.bfloat16
DEGREES = 4
ORDER_PLAN = (3, 1, 2, 0, 4)


def units_of(order):
    return (DEGREES + 2) // 2 if order == 0 else DEGREES + 1 - order


def first_unit(order):
    return sum(units_of(m) for m in range(order))


UNITS = first_unit(DEGREES + 1)


def first_block(order):
    return 0 if order == 0 else DEGREES + 1 + sum(2 * (DEGREES + 1 - m) for m in range(1, order))


def split(value):
    high = value.astype(BF16)
    return high, (value - high.astype(F32)).astype(BF16)


def half_turn(x):
    u = x * x
    s = x * (1 + u * (-1 / 6 + u * (1 / 120 + u * (-1 / 5040 + u * (1 / 362880 - u / 39916800)))))
    c = 1 + u * (
        -0.5
        + u * (1 / 24 + u * (-1 / 720 + u * (1 / 40320 + u * (-1 / 3628800 + u / 479001600))))
    )
    return 1 - 2 * s * s, 2 * s * c


def gelu(x):
    return 0.5 * x * (1 + lax.erf(x * math.sqrt(0.5)))


def dot(a, b):
    return jnp.dot(a, b, preferred_element_type=F32)


def kernel(
    sizes,
    x_ref, pos_ref, esrc_ref, etgt_ref, eang_ref, escale_ref, count_ref, kidx_ref, kfilt_hbm,
    w0_hbm, w1_hbm, w2_hbm, w3_hbm, w4_hbm,
    edge_out, long_out,
    xs, ew, w0, w1, w2, w3, w4, kfilt, y, e, t, h, parts, pair_in, paired, near_in, send, recv,
    x_send, x_recv, ew_send, ew_recv, pair_send, pair_recv, near_send, near_recv, far_send, far_recv, w_sem,
):
    S, T, own, C, rows, sources, edges, kvecs = sizes
    N = S * T
    si, ti = lax.axis_index("src"), lax.axis_index("tgt")
    me = si * T + ti
    hbm = (w0_hbm, w1_hbm, w2_hbm, w3_hbm, w4_hbm)
    held = (w0, w1, w2, w3, w4)
    blocks = (DEGREES + 1) ** 2
    front = (blocks + 1) // 2

    weight_copies = []
    for conv in (0, 1):
        for m in range(DEGREES + 1):
            weight_copies.append(
                pltpu.make_async_copy(hbm[m].at[conv], held[m].at[conv], w_sem.at[conv, m])
            )
    for copy in weight_copies[: DEGREES + 1]:
        copy.start()
    filter_copy = pltpu.make_async_copy(kfilt_hbm, kfilt, w_sem.at[2, 0])

    barrier = pltpu.get_barrier_semaphore()

    far_count = S // 4
    core, near, far = lax.rem(si, 2), lax.rem(si // 2, 2), si // 4
    pair_id, near_id = si + 1 - 2 * core, si + 2 - 4 * near

    def far_id(p):
        return p * 4 + near * 2 + core

    tgt_peers = [lax.rem(ti + d, T) for d in range(1, T)]
    far_peers = [lax.rem(far + d, far_count) for d in range(1, far_count)]
    partners = [(si, p) for p in tgt_peers] + [(pair_id, ti), (near_id, ti)]
    partners += [(far_id(p), ti) for p in far_peers]
    for partner in partners:
        pl.semaphore_signal(barrier, inc=1, device_id=partner, device_id_type=MESH)

    xf = x_ref[...].astype(F32)
    tail = jnp.concatenate(
        [xf[:, front * C :], jnp.zeros((own, (2 * front - blocks) * C), F32)], axis=1
    )
    xs[ti] = jnp.concatenate([xf[:, : front * C], tail], axis=0).astype(BF16)
    lane = lax.broadcasted_iota(jnp.int32, (own, C), 1)
    diagonal = lax.broadcasted_iota(jnp.int32, (own, own), 0) == lax.broadcasted_iota(
        jnp.int32, (own, own), 1
    )
    placed = jnp.zeros((own, C), F32)
    own_columns = []
    for axis in range(3):
        column = jnp.sum(jnp.where(diagonal, pos_ref[axis : axis + 1, :], 0.0), axis=1, keepdims=True)
        own_columns.append(column)
        placed = jnp.where(lane == axis, column, placed)
    ew[me] = jnp.concatenate([xf[:, :C], placed], axis=0)

    pl.semaphore_wait(barrier, len(partners))

    def x_copy(slot, peer, there):
        return pltpu.make_async_remote_copy(
            src_ref=xs.at[slot], dst_ref=xs.at[slot], send_sem=x_send.at[peer],
            recv_sem=x_recv.at[there], device_id=(si, peer), device_id_type=MESH,
        )

    for d in range(1, T):
        x_copy(ti, lax.rem(ti + d, T), ti).start()

    def ew_copy(device, mine, theirs, first, size):
        return pltpu.make_async_remote_copy(
            src_ref=ew.at[pl.ds(first, size)], dst_ref=ew.at[pl.ds(first, size)],
            send_sem=ew_send.at[theirs], recv_sem=ew_recv.at[mine],
            device_id=device, device_id_type=MESH,
        )

    def ew_tgt(p, slot, sem):
        return ew_copy((si, p), sem, p, si * T + slot, 1)

    def ew_pair(owner):
        return ew_copy((pair_id, ti), T, T, owner * T, T)

    def ew_near(owner):
        return ew_copy((near_id, ti), T + 1, T + 1, (owner // 2) * 2 * T, 2 * T)

    def ew_far(p, owner, sem):
        return ew_copy((far_id(p), ti), T + 2 + sem, T + 2 + p, owner * 4 * T, 4 * T)

    for p in tgt_peers:
        ew_tgt(p, ti, ti).start()
    for copy in weight_copies[DEGREES + 1 :]:
        copy.start()
    filter_copy.start()

    c1, s1 = half_turn(0.5 * eang_ref[...])
    c2, s2 = c1 * c1 - s1 * s1, 2 * s1 * c1
    c3, s3 = c2 * c1 - s2 * s1, s2 * c1 + c2 * s1
    c4, s4 = c2 * c2 - s2 * s2, 2 * s2 * c2
    cosines, sines = (None, c1, c2, c3, c4), (None, s1, s2, s3, s4)
    slots = lax.broadcasted_iota(jnp.int32, (1, edges), 1)
    scale = jnp.where(slots < count_ref[ti, si], escale_ref[...], 0.0)
    source_hot = lax.broadcasted_iota(jnp.int32, (sources, edges), 0) == esrc_ref[...]
    target_hot = lax.broadcasted_iota(jnp.int32, (rows, edges), 0) == etgt_ref[...]

    def put(hot, value):
        return jnp.where(hot, value, 0.0)

    def build_e(m):
        if m == 0:
            hot = put(source_hot, jnp.ones((1, edges), F32))
            parts = [hot, hot]
        else:
            ch, sh = cosines[m].astype(BF16).astype(F32), sines[m].astype(BF16).astype(F32)
            ch_hot, sh_hot = put(source_hot, ch), put(source_hot, sh)
            parts = [
                ch_hot, sh_hot, ch_hot, sh_hot,
                put(source_hot, cosines[m] - ch), put(source_hot, sines[m] - sh),
            ]
        depth = e.shape[1]
        used = len(parts) * sources
        if used < depth:
            parts.append(jnp.zeros((depth - used, edges), F32))
        e[...] = jnp.transpose(jnp.concatenate(parts, axis=0)).astype(BF16)

    def build_t(m):
        if m == 0:
            terms = [scale]
        else:
            terms = [scale * cosines[m], scale * sines[m]]
        count = len(terms)
        for i, term in enumerate(terms):
            high = term.astype(BF16).astype(F32)
            t[i * rows : (i + 1) * rows, :] = put(target_hot, high).astype(BF16)
            t[(count + i) * rows : (count + i + 1) * rows, :] = put(target_hot, term - high).astype(BF16)
        return count

    for d in range(1, T):
        peer = lax.rem(ti + d, T)
        x_copy(peer, peer, peer).wait_recv()
    for p in tgt_peers:
        ew_tgt(p, p, p).wait_recv()
    ew_pair(si).start()
    for copy in weight_copies[: DEGREES + 1]:
        copy.wait()
    gathered = xs[...].astype(F32)

    def x_block(index):
        half, at = index // front, index % front
        piece = gathered[:, half * own : (half + 1) * own, at * C : (at + 1) * C]
        return piece.reshape(T * own, C)

    y[...] = jnp.zeros_like(y)
    for m in ORDER_PLAN:
        width = DEGREES + 1 - m
        base = first_block(m)
        if m == 0:
            left = jnp.concatenate([x_block(i) for i in range(width)], axis=1).astype(BF16)
            high, low = split(dot(left, w0[0]))
            for i in range(width):
                at = slice((i % 2) * C, (i % 2 + 1) * C)
                y[i // 2, 0:sources, at] = high[:, i * C : (i + 1) * C]
                y[i // 2, sources : 2 * sources, at] = low[:, i * C : (i + 1) * C]
        else:
            a = jnp.concatenate([x_block(base + i) for i in range(width)], axis=1)
            b = jnp.concatenate([x_block(base + width + i) for i in range(width)], axis=1)
            left = jnp.concatenate([a, b], axis=0).astype(BF16)
            by_w, by_v = dot(left, held[m][0, 0]), dot(left, held[m][0, 1])
            ya = by_w[:sources] - by_v[sources:]
            yb = by_v[:sources] + by_w[sources:]
            ah, al = split(ya)
            bh, bl = split(yb)
            for i in range(width):
                cut = slice(i * C, (i + 1) * C)
                unit = first_unit(m) + i
                for place, (p, q) in enumerate(
                    ((ah, bh), (bh, -ah), (al, bl), (bl, -al), (ah, bh), (bh, -ah))
                ):
                    at = slice(place * sources, (place + 1) * sources)
                    y[unit, at, 0:C] = p[:, cut]
                    y[unit, at, C : 2 * C] = q[:, cut]

    def span(m):
        return pl.ds(first_unit(m), units_of(m))

    def pair_copy(m):
        return pltpu.make_async_remote_copy(
            src_ref=parts.at[:, 1 - core, span(m)], dst_ref=pair_in.at[:, span(m)],
            send_sem=pair_send.at[m], recv_sem=pair_recv.at[m],
            device_id=(pair_id, ti), device_id_type=MESH,
        )

    def near_copy(m):
        return pltpu.make_async_remote_copy(
            src_ref=paired.at[:, 1 - near, span(m)], dst_ref=near_in.at[:, span(m)],
            send_sem=near_send.at[m], recv_sem=near_recv.at[m],
            device_id=(near_id, ti), device_id_type=MESH,
        )

    def far_copy(m, slot, p):
        return pltpu.make_async_remote_copy(
            src_ref=send.at[p, span(m)], dst_ref=recv.at[slot, span(m)],
            send_sem=far_send.at[m, p], recv_sem=far_recv.at[m, slot],
            device_id=(far_id(p), ti), device_id_type=MESH,
        )

    def near_start(m):
        pair_copy(m).wait_recv()

        def add(i, _):
            total = parts[i, core, span(m)].astype(F32) + pair_in[i, span(m)].astype(F32)
            paired[i // 2, lax.rem(i, 2), span(m)] = total.astype(BF16)
            return 0

        lax.fori_loop(0, S // 2, add, 0)
        near_copy(m).start()

    def far_start(m):
        near_copy(m).wait_recv()

        def add(i, _):
            total = paired[i, near, span(m)].astype(F32) + near_in[i, span(m)].astype(F32)
            send[i, span(m)] = total.astype(BF16)
            return 0

        lax.fori_loop(0, far_count, add, 0)
        for d in range(1, far_count):
            p = lax.rem(far + d, far_count)
            far_copy(m, far, p).start()

    step = 256
    for turn, m in enumerate(ORDER_PLAN):
        build_e(m)
        count = build_t(m)

        def one_unit(unit, _, count=count):
            for at in range(0, edges, step):
                h[at : at + step, :] = gelu(dot(e[at : at + step, :], y[unit])).astype(BF16)
            both = dot(t[0 : 2 * count * rows, :], h[...])
            total = both[: count * rows] + both[count * rows :]
            if count == 1:
                a, b = total[:, :C], total[:, C:]
            else:
                a = total[:rows, :C] - total[rows:, C:]
                b = total[:rows, C:] + total[rows:, :C]
            stacked = jnp.concatenate([a.reshape(S, own, C), b.reshape(S, own, C)], axis=1)
            parts[:, :, pl.ds(unit, 1)] = stacked.astype(BF16).reshape(S // 2, 2, 1, 2 * own, C)
            return 0

        lax.fori_loop(first_unit(m), first_unit(m) + units_of(m), one_unit, 0)

        pair_copy(m).start()
        if turn == 0:
            ew_pair(pair_id).wait_recv()
            ew_near(si).start()
        if turn == 1:
            ew_near(near_id).wait_recv()
            for p in far_peers:
                ew_far(p, far, far).start()
        if turn >= 1:
            near_start(ORDER_PLAN[turn - 1])
        if turn >= 2:
            far_start(ORDER_PLAN[turn - 2])

    for p in far_peers:
        ew_far(p, p, p).wait_recv()
    filter_copy.wait()
    k_step = 512
    some = math.gcd(N, 32)

    def tables(columns, at):
        turns = sum(
            column * kidx_ref[axis : axis + 1, pl.ds(at, k_step)].astype(F32)
            for axis, column in enumerate(columns)
        )
        return half_turn(math.pi * (turns - jnp.floor(turns + 0.5)))

    def k_chunk(number, total):
        at = pl.multiple_of(number * k_step, k_step)

        def atoms(group, carried):
            block = ew[pl.ds(group * some, some)]
            charges = jnp.transpose(block[:, :own].reshape(some * own, C)).astype(BF16)
            places = block[:, own:].reshape(some * own, C)
            made = tables([places[:, axis : axis + 1] for axis in range(3)], at)
            return tuple(
                held_sum + sum(dot(charges, part) for part in split(table))
                for held_sum, table in zip(carried, made)
            )

        zero = jnp.zeros((C, k_step), F32)
        if N == some:
            facts_here = atoms(0, (zero, zero))
        else:
            facts_here = lax.fori_loop(0, N // some, atoms, (zero, zero))
        filt = jnp.transpose(kfilt[pl.ds(at, k_step), :])
        for table, fact in zip(tables(own_columns, at), facts_here):
            th, tl = split(table)
            fh, fl = split(filt * fact)
            dims = (((1,), (1,)), ((), ()))
            for p, q in ((th, fh), (tl, fh), (th, fl)):
                total = total + lax.dot_general(p, q, dims, preferred_element_type=F32)
        return total

    chunks = kvecs // k_step
    summed = lax.fori_loop(0, chunks // 2, k_chunk, jnp.zeros((own, C), F32))
    near_start(ORDER_PLAN[-1])
    far_start(ORDER_PLAN[-2])
    summed = lax.fori_loop(chunks // 2, chunks - chunks // 4, k_chunk, summed)
    far_start(ORDER_PLAN[-1])
    summed = lax.fori_loop(chunks - chunks // 4, chunks, k_chunk, summed)
    long_out[...] = summed * (1.0 / math.sqrt(N * own * kvecs))

    for copy in weight_copies[DEGREES + 1 :]:
        copy.wait()
    for m in ORDER_PLAN:

        total = send[far, span(m)].astype(F32)
        for d in range(1, far_count):
            p = lax.rem(far + d, far_count)
            far_copy(m, p, p).wait_recv()
            total = total + recv[p, span(m)].astype(F32)
        width = DEGREES + 1 - m
        base = first_block(m) * C
        if m == 0:
            left = jnp.concatenate(
                [total[i // 2, (i % 2) * own : (i % 2 + 1) * own] for i in range(width)], axis=1
            )
            by_w = dot(jnp.concatenate(split(left), axis=0), w0[1])
            edge_out[:, : width * C] = (by_w[:own] + by_w[own:]).astype(BF16)
        else:
            left = jnp.concatenate([total[i] for i in range(width)], axis=1)
            left = jnp.concatenate(split(left), axis=0)
            by_w, by_v = dot(left, held[m][1, 0]), dot(left, held[m][1, 1])
            by_w, by_v = (v[: 2 * own] + v[2 * own :] for v in (by_w, by_v))
            edge_out[:, base : base + width * C] = (by_w[:own] - by_v[own:]).astype(BF16)
            edge_out[:, base + width * C : base + 2 * width * C] = (by_v[:own] + by_w[own:]).astype(BF16)

    for d in range(1, T):
        peer = lax.rem(ti + d, T)
        x_copy(ti, peer, ti).wait_send()

    for p in tgt_peers:
        ew_tgt(p, ti, ti).wait_send()
    ew_pair(si).wait_send()
    ew_near(si).wait_send()
    for p in far_peers:
        ew_far(p, far, far).wait_send()
    for m in ORDER_PLAN:
        pair_copy(m).wait_send()
        near_copy(m).wait_send()
        for d in range(1, far_count):
            far_copy(m, far, lax.rem(far + d, far_count)).wait_send()


def hand_on(edge_in, long_in, edge_out, long_out):
    edge_out[...] = edge_in[...]
    long_out[...] = long_in[...]


def body(
    atom_feats, positions, edge_src, edge_tgt, edge_angle, edge_scale, edge_count, k_index, k_filter,
    weight_zero, weight_first, weight_second, weight_third, weight_fourth,
):
    S, T = lax.axis_size("src"), lax.axis_size("tgt")
    own, features = atom_feats.shape
    kvecs, C = k_filter.shape
    edges = edge_src.shape[0]
    rows, sources = own * S, own * T
    weights = (weight_zero, weight_first, weight_second, weight_third, weight_fourth)
    sizes = (S, T, own, C, rows, sources, edges, kvecs)
    depth = max(C, 6 * sources)
    front = ((DEGREES + 1) ** 2 + 1) // 2
    vmem = pl.BlockSpec(memory_space=pltpu.VMEM)
    smem = pl.BlockSpec(memory_space=pltpu.SMEM)
    anywhere = pl.BlockSpec(memory_space=pl.ANY)
    dma = pltpu.SemaphoreType.DMA
    row = lambda v: v.reshape(1, edges)
    made = pl.pallas_call(
        functools.partial(kernel, sizes),
        out_shape=(
            jax.ShapeDtypeStruct((own, features), BF16),
            jax.ShapeDtypeStruct((own, C), F32),
        ),
        in_specs=[vmem] * 6 + [smem, vmem] + [anywhere] * 6,
        out_specs=(vmem, vmem),
        scratch_shapes=[
            pltpu.VMEM((T, 2 * own, front * C), BF16),
            pltpu.VMEM((S * T, 2 * own, C), F32),
            *[pltpu.VMEM(w.shape, BF16) for w in weights],
            pltpu.VMEM((kvecs, C), F32),
            pltpu.VMEM((UNITS, depth, 2 * C), BF16),
            pltpu.VMEM((edges, depth), BF16),
            pltpu.VMEM((4 * rows, edges), BF16),
            pltpu.VMEM((edges, 2 * C), BF16),
            pltpu.VMEM((S // 2, 2, UNITS, 2 * own, C), BF16),
            pltpu.VMEM((S // 2, UNITS, 2 * own, C), BF16),
            pltpu.VMEM((S // 4, 2, UNITS, 2 * own, C), BF16),
            pltpu.VMEM((S // 4, UNITS, 2 * own, C), BF16),
            pltpu.VMEM((S // 4, UNITS, 2 * own, C), BF16),
            pltpu.VMEM((S // 4, UNITS, 2 * own, C), BF16),
            dma((T,)), dma((T,)), dma((T + 2 + S // 4,)), dma((T + 2 + S // 4,)),
            *[dma((DEGREES + 1,)) for _ in range(4)],
            dma((DEGREES + 1, S // 4)), dma((DEGREES + 1, S // 4)), dma((3, DEGREES + 1)),
        ],
        compiler_params=pltpu.CompilerParams(
            collective_id=0, has_side_effects=True, vmem_limit_bytes=56 * 1024 * 1024
        ),
    )(
        atom_feats, positions, row(edge_src), row(edge_tgt), row(edge_angle), row(edge_scale),
        edge_count.T, k_index, k_filter, *weights,
    )
    return pl.pallas_call(
        hand_on,
        out_shape=tuple(jax.ShapeDtypeStruct(v.shape, v.dtype) for v in made),
        in_specs=[vmem, vmem],
        out_specs=(vmem, vmem),
    )(*made)


def solution(mesh):
    both = P(("src", "tgt"))
    return jax.shard_map(
        body,
        mesh=mesh,
        in_specs=(
            P(("src", "tgt"), None), P(None, ("src", "tgt")), both, both, both, both,
            P(), P(), P(), P(), P(), P(), P(), P(),
        ),
        out_specs=(P(("tgt", "src"), None), P(("src", "tgt"), None)),
        check_vma=False,
    )
```
